256 devices in a mesh: seq: 64 (over y, z, core), kvh: 4 (over x).
Axes of the slice: x: 4, y: 4, z: 8, core: 2. Of those that a mesh axis runs over, the one named last changes fastest.
Arguments:
- queries: bfloat16 [32768, 4096], P('seq', 'kvh'), may hold values from -30 to 30
- keys: bfloat16 [32768, 512], P('seq', 'kvh'), may hold values from -6 to 6
- values: bfloat16 [32768, 512], P('seq', 'kvh'), may hold values from -6 to 6
- attn_out: bfloat16 [32768, 4096], P('seq', 'kvh'), may hold values from -6 to 6
- out_grad: bfloat16 [32768, 4096], P('seq', 'kvh'), may hold values from -6 to 6
- episode_ids: int32 [32768], P('seq'), may hold values from 0 to 31, never falling along the last dimension, each value on 1 to 8192 neighbouring positions
- key_proj: bfloat16 [8192, 512], P('kvh'), may hold values from -0.25 to 0.25
- value_proj: bfloat16 [8192, 512], P('kvh'), may hold values from -0.25 to 0.25
Outputs:
- query_grad: bfloat16 [32768, 4096], P('seq', 'kvh')
- key_grad: bfloat16 [32768, 512], P('seq', 'kvh')
- value_grad: bfloat16 [32768, 512], P('seq', 'kvh')
- input_grad: bfloat16 [32768, 8192], P('seq', 'kvh')
The draws below stay inside these ranges and needn't reach their ends.
Inputs may be any that keep to these rules, and one draw needn't show every extreme that they name: `episode_ids`: episode ids never fall along the sequence; every episode is 1 to 8192 consecutive tokens and one has exactly 8192.
All inputs are finite; a program needn't handle non-finite values.
Results may differ from the reference program's by a relative error of at most 0.006.
Values may be sent and summed in bfloat16 or wider, within the bound.
No kernel may reach another device: no remote copies, remote signals or barrier semaphores. Data moves between devices by JAX's collectives and lax.ppermute only.
A program may use at most 128 MiB of HBM per device.

```python
import math
import jax
import jax.numpy as jnp
import numpy as np
from jax import lax

D = 8192
H = 32
KVH = 4
HD = 128
G = 8
TOK_DEV = 512
SEQ = 32768
EP_MAX = 8192
NEP = 32


def draw_keys(key, part):
    key = jax.random.fold_in(key, 3)
    result = jax.random.truncated_normal(key, -6.0, 6.0, (SEQ, KVH * HD), jnp.float32)
    return result.astype(jnp.bfloat16)


def draw_queries(key, part):
    key = jax.random.fold_in(key, 5)
    result = jax.random.truncated_normal(key, -6.0, 6.0, (SEQ, H * HD), jnp.float32)
    return result.astype(jnp.bfloat16)


def steps_of(key, extent, pieces, least, largest):
    gain = 1.0
    for axis_at, blocks in pieces:
        steps = jax.random.uniform(jax.random.fold_in(jax.random.fold_in(key, 6), axis_at), (blocks,), jnp.float32, least / len(pieces), largest / len(pieces))
        gain = gain * jnp.repeat(jnp.exp(steps), extent[axis_at] // blocks).reshape((-1,) + (1,) * (len(extent) - 1 - axis_at))
    return gain


def split_up(count, total, most, lean):
    loads = [(1 << 20) // math.isqrt(grade ** lean) + 1 for grade in range(2, count + 1)]
    spare, given = total - most - (count - 1), [1] * (count - 1)
    while spare > 0:
        candidates = [i for i in range(count - 1) if given[i] < most]
        pool, remaining = sum([loads[i] for i in candidates]), spare
        for i in candidates:
            more = min(most - given[i], max(1, remaining * loads[i] // pool), spare)
            given[i] = given[i] + more
            spare = spare - more
    return np.array([most] + given)


def uneven(key, amount, total, most, skew):
    if amount == 2:
        one = jax.random.randint(key, (), max(1, total - most), min(most, total - 1) + 1)
        return jnp.stack([one, total - one])
    tallies = jnp.asarray(split_up(amount, total, most, skew), jnp.int32)
    pairs = (amount - 1) // 2
    donor, receiver = tallies[1:1 + 2 * pairs:2], tallies[2:2 + 2 * pairs:2]
    room = jnp.minimum(donor - 1, most - receiver)
    passed = jax.random.randint(jax.random.fold_in(key, 1), (pairs,), 0, 1 << 20) % (room + 1)
    tallies = tallies.at[1:1 + 2 * pairs:2].set(donor - passed).at[2:2 + 2 * pairs:2].set(receiver + passed)
    return tallies[jax.random.permutation(jax.random.fold_in(key, 2), amount)]


def normal_values(stream_key, extent, scale, most, pieces=(), kind=jnp.bfloat16):
    values = scale * jax.random.normal(stream_key, extent, jnp.float32)
    if pieces:
        values = values * steps_of(stream_key, extent, pieces, -0.22, 0.18)
    return jnp.clip(values, -most, most).astype(kind)


def setup_inputs(seed: int = 0) -> dict:
    splits = jax.random.split(jax.random.key(seed), 9)
    return {
        "queries": draw_queries(jax.random.fold_in(splits[8], 71), 0),
        "keys": draw_keys(jax.random.fold_in(splits[8], 71), 0),
        "values": normal_values(splits[2], (SEQ, KVH * HD), 1.0, 6.0, ((0, 64), (1, 4))),
        "attn_out": normal_values(splits[3], (SEQ, H * HD), 1.0, 6.0, ((0, 64), (1, 4))),
        "out_grad": normal_values(splits[4], (SEQ, H * HD), 1.0, 6.0, ((0, 64), (1, 4))),
        "episode_ids": jnp.searchsorted(jnp.cumsum(uneven(splits[5], NEP, SEQ, EP_MAX, 2)), jnp.arange(SEQ), side="right").astype(jnp.int32),
        "key_proj": normal_values(splits[6], (D, KVH * HD), (KVH * HD) ** -0.5, 0.25, ((0, 4),)),
        "value_proj": normal_values(splits[7], (D, KVH * HD), (KVH * HD) ** -0.5, 0.25, ((0, 4),)),
    }


def reference(queries, keys, values, attn_out, out_grad, episode_ids, key_proj, value_proj):
    scale = HD ** -0.5
    reach = (EP_MAX + TOK_DEV - 2) // TOK_DEV
    margin = reach * TOK_DEV
    width = margin + TOK_DEV
    key_pad = jnp.concatenate([jnp.zeros((margin, KVH * HD), keys.dtype), keys], 0)
    value_pad = jnp.concatenate([jnp.zeros((margin, KVH * HD), values.dtype), values], 0)
    ident_pad = jnp.concatenate([jnp.full((margin,), -1, jnp.int32), episode_ids.astype(jnp.int32)], 0)
    blocks = SEQ // TOK_DEV

    def step(carry, block):
        key_acc, value_acc = carry
        start = (block * TOK_DEV).astype(jnp.int32)
        query_rows = lax.dynamic_slice_in_dim(queries, start, TOK_DEV, 0)
        grad_rows = lax.dynamic_slice_in_dim(out_grad, start, TOK_DEV, 0)
        out_rows = lax.dynamic_slice_in_dim(attn_out, start, TOK_DEV, 0)
        ident_rows = lax.dynamic_slice_in_dim(episode_ids, start, TOK_DEV, 0)
        key_win = lax.dynamic_slice_in_dim(key_pad, start, width, 0)
        value_win = lax.dynamic_slice_in_dim(value_pad, start, width, 0)
        ident_win = lax.dynamic_slice_in_dim(ident_pad, start, width, 0)
        query_pos = start + jnp.arange(TOK_DEV, dtype=jnp.int32)
        key_pos = start - margin + jnp.arange(width, dtype=jnp.int32)
        visible = (ident_rows[:, None] == ident_win[None, :]) & (key_pos[None, :] <= query_pos[:, None])
        query_parts, key_parts, value_parts = [], [], []
        for group_idx in range(KVH):
            cols = slice(group_idx * G * HD, (group_idx + 1) * G * HD)
            query_h = query_rows[:, cols].reshape(TOK_DEV, G, HD).astype(jnp.float32)
            grad_h = grad_rows[:, cols].reshape(TOK_DEV, G, HD).astype(jnp.float32)
            out_h = out_rows[:, cols].reshape(TOK_DEV, G, HD).astype(jnp.float32)
            key_h = key_win[:, group_idx * HD:(group_idx + 1) * HD].astype(jnp.float32)
            value_h = value_win[:, group_idx * HD:(group_idx + 1) * HD].astype(jnp.float32)
            scores = scale * jnp.einsum('tgd,sd->gts', query_h, key_h)
            top = jnp.max(jnp.where(visible[None], scores, -1e30), -1)
            total = jnp.sum(jnp.where(visible[None], jnp.exp(scores - top[..., None]), 0.0), -1)
            lse = top + jnp.log(total)
            probs = jnp.where(visible[None], jnp.exp(scores - lse[..., None]), 0.0)
            probs_b = lax.optimization_barrier(probs.astype(jnp.bfloat16)).astype(jnp.float32)
            value_parts.append(jnp.einsum('gts,tgd->sd', probs_b, grad_h))
            dprobs = jnp.einsum('tgd,sd->gts', grad_h, value_h)
            delta = jnp.sum(grad_h * out_h, -1).T
            dscore = probs * (dprobs - delta[:, :, None])
            dscore_b = lax.optimization_barrier(dscore.astype(jnp.bfloat16)).astype(jnp.float32)
            query_parts.append((scale * jnp.einsum('gts,sd->tgd', dscore_b, key_h)).reshape(TOK_DEV, G * HD))
            key_parts.append(scale * jnp.einsum('gts,tgd->sd', dscore_b, query_h))
        key_add = jnp.concatenate(key_parts, 1)
        value_add = jnp.concatenate(value_parts, 1)
        key_acc = lax.dynamic_update_slice_in_dim(key_acc, lax.dynamic_slice_in_dim(key_acc, start, width, 0) + key_add, start, 0)
        value_acc = lax.dynamic_update_slice_in_dim(value_acc, lax.dynamic_slice_in_dim(value_acc, start, width, 0) + value_add, start, 0)
        return (key_acc, value_acc), jnp.concatenate(query_parts, 1).astype(jnp.bfloat16)

    init = (jnp.zeros((margin + SEQ, KVH * HD), jnp.float32), jnp.zeros((margin + SEQ, KVH * HD), jnp.float32))
    (key_acc, value_acc), query_blocks = lax.scan(step, init, jnp.arange(blocks, dtype=jnp.int32))
    query_grad = query_blocks.reshape(SEQ, H * HD)
    key_grad = key_acc[margin:].astype(jnp.bfloat16)
    value_grad = value_acc[margin:].astype(jnp.bfloat16)
    input_grad = jnp.dot(key_grad, key_proj.T, preferred_element_type=jnp.float32) + jnp.dot(value_grad, value_proj.T, preferred_element_type=jnp.float32)
    return query_grad, key_grad, value_grad, input_grad.astype(jnp.bfloat16)
```

```python
import functools
import math
import jax
import jax.numpy as jnp
from jax import lax
from jax.experimental import pallas as pl
from jax.experimental.pallas import tpu as pltpu
from jax.sharding import PartitionSpec as P

HEAD = 128
EPISODES = 32
LOG2E = 1.4426950408889634
NT = (((1,), (1,)), ((), ()))
NN = (((1,), (0,)), ((), ()))
QT = 256


def dot(a, b, dims):
    return lax.dot_general(a, b, dims, preferred_element_type=jnp.float32)


def seen(base, start, q_at, causal):
    place = lax.broadcasted_iota(jnp.int32, (start.shape[0], start.shape[1]), 0) + base
    mask = place >= start
    if causal:
        mask = mask & (place <= lax.broadcasted_iota(jnp.int32, start.shape, 1) + q_at)
    return mask


def tile_live(base, rows, first_start, q_at, causal):
    live = base + rows > first_start
    if causal:
        live = live & (base < q_at + QT)
    return live


def stat_kernel(blocks, causal, first, *refs):
    base_ref, low_ref, start_ref, q_ref = refs[:4]
    kv_refs = refs[4 : 4 + blocks]
    if first:
        top_ref, sum_ref = refs[4 + blocks :]
        top_ref[...] = jnp.full(top_ref.shape, -1e30, jnp.float32)
        sum_ref[...] = jnp.zeros(sum_ref.shape, jnp.float32)
    else:
        top_in, sum_in, top_ref, sum_ref = refs[4 + blocks :]
        top_ref[...] = top_in[...]
        sum_ref[...] = sum_in[...]
    rows = q_ref.shape[0]
    heads = q_ref.shape[1] // HEAD
    gain = HEAD ** (-0.5) * LOG2E
    for block in range(blocks):
        base = base_ref[block]
        for part in range(rows // QT):
            cols = pl.ds(part * QT, QT)

            @pl.when(tile_live(base, rows, low_ref[part], part * QT, causal))
            def _():
                def one(head):
                    lanes = pl.ds(pl.multiple_of(head * HEAD, HEAD), HEAD)
                    scores = gain * dot(kv_refs[block][:, :HEAD], q_ref[cols, lanes], NT)
                    start = jnp.broadcast_to(start_ref[:, cols], scores.shape)
                    scores = jnp.where(seen(base, start, part * QT, causal), scores, -1e30)
                    top = top_ref[pl.ds(head, 1), cols]
                    new_top = jnp.maximum(top, jnp.max(scores, 0, keepdims=True))
                    add = jnp.sum(jnp.exp2(scores - new_top), 0, keepdims=True)
                    add = jnp.where(new_top > -1e29, add, 0.0)
                    sum_ref[pl.ds(head, 1), cols] = (
                        sum_ref[pl.ds(head, 1), cols] * jnp.exp2(top - new_top) + add
                    )
                    top_ref[pl.ds(head, 1), cols] = new_top

                def pair(step, _):
                    one(2 * step)
                    one(2 * step + 1)
                    return 0

                lax.fori_loop(0, heads // 2, pair, 0)


def grad_kernel(blocks, causal, first, last, *refs):
    base_ref, low_ref, start_ref, q_ref, g_ref, top_ref, sum_ref, delta_ref = refs[:8]
    kv_refs = refs[8 : 8 + blocks]
    rest = refs[8 + blocks :]
    rows = q_ref.shape[0]
    heads = q_ref.shape[1] // HEAD
    scale = HEAD ** (-0.5)
    gain = scale * LOG2E
    if first:
        acc_in = None
    else:
        acc_in, rest = rest[0], rest[1:]
    out_refs, rest = rest[:blocks], rest[blocks:]
    if last:
        dq_ref, acc_ref, lse_ref = rest
    else:
        acc_ref, lse_ref = rest
    if first:
        acc_ref[...] = jnp.zeros(acc_ref.shape, jnp.float32)
    else:
        acc_ref[...] = acc_in[...]
    lse_ref[...] = top_ref[...] + jnp.log2(sum_ref[...])
    for block in range(blocks):
        base = base_ref[block]
        out_refs[block][...] = jnp.zeros(out_refs[block].shape, jnp.float32)
        for part in range(rows // QT):
            cols = pl.ds(part * QT, QT)

            @pl.when(tile_live(base, rows, low_ref[part], part * QT, causal))
            def _():
                keys = kv_refs[block][:, :HEAD]
                keys_t = keys.T

                def one(head):
                    lanes = pl.ds(pl.multiple_of(head * HEAD, HEAD), HEAD)
                    query = q_ref[cols, lanes]
                    grad = g_ref[cols, lanes]
                    scores = gain * dot(keys, query, NT)
                    dprobs = dot(kv_refs[block][:, HEAD:], grad, NT)
                    start = jnp.broadcast_to(start_ref[:, cols], scores.shape)
                    probs = jnp.exp2(scores - lse_ref[pl.ds(head, 1), cols])
                    probs = jnp.where(seen(base, start, part * QT, causal), probs, 0.0)
                    dscores = probs * (dprobs - delta_ref[pl.ds(head, 1), cols])
                    probs_b = probs.astype(jnp.bfloat16)
                    dscores_b = dscores.astype(jnp.bfloat16)
                    acc_ref[head, :, cols] += dot(keys_t, dscores_b, NN)
                    return dot(dscores_b, query, NN), dot(probs_b, grad, NN)

                def pair(step, _):
                    key_a, value_a = one(2 * step)
                    key_b, value_b = one(2 * step + 1)
                    out_refs[block][:, :HEAD] += key_a + key_b
                    out_refs[block][:, HEAD:] += value_a + value_b
                    return 0

                lax.fori_loop(0, heads // 2, pair, 0)

    if last:
        for head in range(heads):
            dq_ref[:, head * HEAD : (head + 1) * HEAD] = (scale * acc_ref[head].T).astype(dq_ref.dtype)


SMEM = functools.partial(pl.BlockSpec, memory_space=pltpu.SMEM)
VMEM = functools.partial(pl.BlockSpec, memory_space=pltpu.VMEM)
PARAMS = pltpu.CompilerParams(vmem_limit_bytes=48 * 2**20)


def stat_call(bases, lows, start, queries, blocks, causal, stats):
    heads, rows = queries.shape[1] // HEAD, queries.shape[0]
    count = len(blocks)
    shape = jax.ShapeDtypeStruct((heads, rows), jnp.float32)
    extra = () if stats is None else tuple(stats)
    return pl.pallas_call(
        functools.partial(stat_kernel, count, causal, stats is None),
        out_shape=(shape, shape),
        in_specs=[SMEM(), SMEM()] + [VMEM()] * (2 + count + len(extra)),
        out_specs=(VMEM(), VMEM()),
        compiler_params=PARAMS,
        cost_estimate=pl.CostEstimate(
            flops=4 * count * heads * rows * rows * HEAD,
            bytes_accessed=queries.size * 2 + count * rows * HEAD * 4,
            transcendentals=0,
        ),
        name="stats",
    )(bases, lows, start, queries, *blocks, *extra)


def grad_call(bases, lows, start, queries, grads, stats, delta, blocks, causal, acc, last):
    heads, rows = queries.shape[1] // HEAD, queries.shape[0]
    count = len(blocks)
    extra = () if acc is None else (acc,)
    acc_shape = jax.ShapeDtypeStruct((heads, HEAD, rows), jnp.float32)
    out_shape = [jax.ShapeDtypeStruct((rows, 2 * HEAD), jnp.float32)] * count
    scratch = [pltpu.VMEM((heads, rows), jnp.float32)]
    if last:
        out_shape.append(jax.ShapeDtypeStruct(queries.shape, jnp.bfloat16))
        scratch = [pltpu.VMEM(acc_shape.shape, jnp.float32)] + scratch
    else:
        out_shape.append(acc_shape)
    return pl.pallas_call(
        functools.partial(grad_kernel, count, causal, acc is None, last),
        out_shape=tuple(out_shape),
        in_specs=[SMEM(), SMEM()] + [VMEM()] * (6 + count + len(extra)),
        out_specs=tuple([VMEM()] * len(out_shape)),
        scratch_shapes=scratch,
        compiler_params=PARAMS,
        cost_estimate=pl.CostEstimate(
            flops=20 * count * heads * rows * rows * HEAD,
            bytes_accessed=queries.size * 4 + count * rows * HEAD * 16,
            transcendentals=0,
        ),
        name="grads",
    )(bases, lows, start, queries, grads, *stats, delta, *blocks, *extra)


def shift(value, steps):
    count = lax.axis_size("seq")
    return lax.ppermute(value, "seq", [(i, (i + steps) % count) for i in range(count)])


def swap(value):
    return lax.ppermute(value, "seq", [(i, i ^ 1) for i in range(lax.axis_size("seq"))])


def per_device(queries, keys, values, attn_out, out_grad, episode_ids, key_proj, value_proj):
    rows = queries.shape[0]
    group = queries.shape[1] // HEAD
    scale = HEAD ** (-0.5)
    shard = lax.axis_index("seq")
    core = shard % 2

    counts = jnp.sum(episode_ids[None, :] == jnp.arange(EPISODES)[:, None], 1, dtype=jnp.int32)
    all_counts = lax.all_gather(counts, "seq")
    earlier = jnp.arange(lax.axis_size("seq"))[:, None] < shard
    ours = jnp.arange(EPISODES)[None, :] == episode_ids[0]
    before = jnp.sum(jnp.where(earlier & ours, all_counts, 0), dtype=jnp.int32)
    local = jnp.sum(episode_ids[None, :] < episode_ids[:, None], 1, dtype=jnp.int32)
    start = jnp.where(episode_ids == episode_ids[0], -before, local)
    lows = start[::QT]
    start = start[None, :]

    kv = jnp.concatenate([keys, values], 1)
    own = {0: kv}
    own[8] = shift(kv, 16)
    for near, far in ((1, 7), (2, 6), (3, 5)):
        own[near] = shift(own[near - 1], 2)
        own[far] = shift(own[far + 1], -2)
    own[4] = shift(own[3], 2)
    other = {d: swap(own[d]) for d in range(9)}
    sides = 1 - 2 * core

    def bases_of(distances):
        steps = []
        for d in distances:
            steps += [jnp.int32(-2 * d), sides - 2 * d]
        return jnp.stack(steps).astype(jnp.int32) * rows

    def blocks_of(distances):
        found = []
        for d in distances:
            found += [own[d], other[d]]
        return found

    groups = ((5, 4), (6, 3), (7, 2), (8, 1))
    stats = None
    for distances in ((0,),) + groups[::-1]:
        stats = stat_call(
            bases_of(distances), lows, start, queries, blocks_of(distances), 0 in distances, stats
        )
    grad_3 = out_grad.reshape(rows, group, HEAD).astype(jnp.float32)
    delta = jnp.sum(grad_3 * attn_out.reshape(rows, group, HEAD).astype(jnp.float32), -1).T

    acc = None
    far_sum = near_sum = None
    for distances in groups:
        far_own, far_other, near_own, near_other, acc = grad_call(
            bases_of(distances), lows, start, queries, out_grad, stats, delta,
            blocks_of(distances), False, acc, False,
        )
        far_part = far_own + swap(far_other)
        near_part = near_own + swap(near_other)
        if far_sum is not None:
            far_part = far_part + far_sum
            near_part = near_part + near_sum
        far_sum = shift(far_part, 2 if distances[0] < 8 else -16)
        near_sum = shift(near_part, -2)
    part, part_other, query_grad = grad_call(
        bases_of((0,)), lows, start, queries, out_grad, stats, delta, blocks_of((0,)), True, acc, True
    )
    total = part + swap(part_other) + far_sum + near_sum
    key_grad = (scale * total[:, :HEAD]).astype(jnp.bfloat16)
    value_grad = total[:, HEAD:].astype(jnp.bfloat16)
    all_key_grad = lax.all_gather(key_grad, "kvh", axis=1, tiled=True)
    all_value_grad = lax.all_gather(value_grad, "kvh", axis=1, tiled=True)
    input_grad = dot(all_key_grad, key_proj, NT) + dot(all_value_grad, value_proj, NT)
    return query_grad, key_grad, value_grad, input_grad.astype(jnp.bfloat16)


def solution(mesh):
    in_specs = (
        P("seq", "kvh"),
        P("seq", "kvh"),
        P("seq", "kvh"),
        P("seq", "kvh"),
        P("seq", "kvh"),
        P("seq"),
        P("kvh", None),
        P("kvh", None),
    )
    out_specs = (P("seq", "kvh"), P("seq", "kvh"), P("seq", "kvh"), P("seq", "kvh"))
    return jax.shard_map(
        per_device, mesh=mesh, in_specs=in_specs, out_specs=out_specs, check_vma=False
    )
```

```python
import functools
import jax
import jax.numpy as jnp
from jax import lax
from jax.experimental import pallas as pl
from jax.experimental.pallas import tpu as pltpu
from jax.sharding import PartitionSpec as P

HEAD = 128
LOG2E = 1.4426950408889634
SCALE = HEAD ** (-0.5)
GAIN = SCALE * LOG2E
NT = (((1,), (1,)), ((), ()))
NN = (((1,), (0,)), ((), ()))
QT = 256
JOIN = 4
META = 16
BOUND = 50.0


def dot(a, b, dims):
    return lax.dot_general(a, b, dims, preferred_element_type=jnp.float32)


def head_lanes(head):
    return pl.ds(pl.multiple_of(head * HEAD, HEAD), HEAD)


def pack_kernel(ids_ref, k_ref, v_ref, out_ref):
    rows = k_ref.shape[0]
    out_ref[:rows, :HEAD] = k_ref[...]
    out_ref[:rows, HEAD:] = v_ref[...]
    keys = k_ref[...].astype(jnp.float32)
    norm = 1.01 * jnp.max(jnp.sum(keys * keys, 1, keepdims=True))
    ids = ids_ref[...].astype(jnp.float32)
    last = jnp.max(ids)
    run = jnp.sum(jnp.where(ids == last, 1.0, 0.0)).astype(jnp.int32)
    lane = lax.broadcasted_iota(jnp.int32, (META, 2 * HEAD), 1)
    meta = jnp.where(lane == 0, last, jnp.where(lane == 1, (run >> 1).astype(jnp.float32), 0.0))
    meta = jnp.where(lane == 2, (run & 1).astype(jnp.float32), jnp.where(lane == 3, norm, meta))
    out_ref[rows:, :] = meta.astype(jnp.bfloat16)


def delta_kernel(q_ref, g_ref, o_ref, delta_ref, norm_ref):
    heads = delta_ref.shape[0]
    norm = jnp.float32(0.0)
    for head in range(heads):
        lanes = slice(head * HEAD, (head + 1) * HEAD)
        product = g_ref[:, lanes].astype(jnp.float32) * o_ref[:, lanes].astype(jnp.float32)
        high = product.astype(jnp.bfloat16)
        low = (product - high.astype(jnp.float32)).astype(jnp.bfloat16)
        both = jnp.concatenate([high, low], 1)
        delta_ref[head : head + 1, :] = dot(jnp.ones((16, 2 * HEAD), jnp.bfloat16), both, NT)[:1]
        query = q_ref[:, lanes].astype(jnp.float32)
        square = (query * query).astype(jnp.bfloat16)
        norm = jnp.maximum(norm, jnp.max(dot(jnp.ones((16, HEAD), jnp.bfloat16), square, NT)))
    norm_ref[0] = 1.02 * norm


def own_mask(local_ref, keys, part):
    shape = (keys, QT)
    place = lax.broadcasted_iota(jnp.int32, shape, 0)
    query = lax.broadcasted_iota(jnp.int32, shape, 1) + part * QT
    return (place >= local_ref[:, part * QT : (part + 1) * QT]) & (place <= query)


def past_mask(rows, low, first_run, part):
    shape = (rows, QT)
    place = lax.broadcasted_iota(jnp.int32, shape, 0)
    query = lax.broadcasted_iota(jnp.int32, shape, 1) + part * QT
    return (place >= low) & (query < first_run)


def stat_general(keys, mask, q_ref, part, state_ref, heads):
    cols = pl.ds(part * QT, QT)

    def one(head, _):
        row = pl.ds(head, 1)
        scores = GAIN * dot(keys, q_ref[cols, head_lanes(head)], NT)
        scores = jnp.where(mask, scores, -1e30)
        top = state_ref[0, row, cols]
        new_top = jnp.maximum(top, jnp.max(scores, 0, keepdims=True))
        add = jnp.sum(jnp.exp2(scores - new_top), 0, keepdims=True)
        add = jnp.where(new_top > -1e29, add, 0.0)
        state_ref[1, row, cols] = state_ref[1, row, cols] * jnp.exp2(top - new_top) + add
        state_ref[0, row, cols] = new_top
        return 0

    lax.fori_loop(0, heads, one, 0)


def stat_bounded(keys, q_ref, part, state_ref, heads):
    cols = pl.ds(part * QT, QT)

    def some(step, _):
        for at in range(JOIN):
            head = step * JOIN + at
            powers = jnp.exp2(GAIN * dot(keys, q_ref[cols, head_lanes(head)], NT))
            state_ref[2, pl.ds(head, 1), cols] += jnp.sum(powers, 0, keepdims=True)
        return 0

    lax.fori_loop(0, heads // JOIN, some, 0)


def stat_own_kernel(local_ref, q_ref, kv_ref, state_ref):
    heads, rows = state_ref.shape[1], state_ref.shape[2]
    state_ref[0] = jnp.full((heads, rows), -1e30, jnp.float32)
    state_ref[1] = jnp.zeros((heads, rows), jnp.float32)
    state_ref[2] = jnp.zeros((heads, rows), jnp.float32)
    for part in range(rows // QT):
        upto = (part + 1) * QT
        stat_general(
            kv_ref[:upto, :HEAD], own_mask(local_ref, upto, part), q_ref, part, state_ref, heads
        )


def stat_past_kernel(count, seen_ref, first_ref, key_norm_ref, norm_ref, q_ref, *refs):
    kv_refs, (state_in, state_ref, keys_ref) = refs[:count], refs[count:]
    heads, rows = state_ref.shape[1], state_ref.shape[2]
    state_ref[...] = state_in[...]
    for block in range(count):
        keys_ref[block] = kv_refs[block][:rows, :HEAD]

    def one_block(block, _):
        seen, first_run = seen_ref[block], first_ref[0]
        bounded = key_norm_ref[block] * norm_ref[0] * (GAIN * GAIN) < BOUND * BOUND
        for part in range(rows // QT):
            live = (seen > 0) & (first_run > part * QT)
            whole = (seen == rows) & (first_run >= (part + 1) * QT) & bounded

            @pl.when(live & whole)
            def _():
                stat_bounded(keys_ref[block], q_ref, part, state_ref, heads)

            @pl.when(live & jnp.logical_not(whole))
            def _():
                mask = past_mask(rows, rows - seen, first_run, part)
                stat_general(keys_ref[block], mask, q_ref, part, state_ref, heads)

        return 0

    lax.fori_loop(0, count, one_block, 0)


def lse_of(state_ref):
    top, total, flat = state_ref[0], state_ref[1], state_ref[2]
    flat_log = jnp.where(flat > 0, jnp.log2(jnp.where(flat > 0, flat, 1.0)), -1e30)
    high = jnp.maximum(top, flat_log)
    return high + jnp.log2(total * jnp.exp2(top - high) + jnp.exp2(flat_log - high))


def grad_tile(kv_ref, keys_t, keys, mask, part, refs, out_ref):
    q_ref, g_ref, delta_ref, lse_ref, acc_ref = refs
    heads = lse_ref.shape[0]
    cols = pl.ds(part * QT, QT)

    def some(step, _):
        probs_list, dscores_list, query_list, grad_list = [], [], [], []
        for at in range(JOIN):
            head = step * JOIN + at
            row = pl.ds(head, 1)
            query = q_ref[cols, head_lanes(head)]
            grad = g_ref[cols, head_lanes(head)]
            scores = GAIN * dot(kv_ref[:keys, :HEAD], query, NT)
            dprobs = dot(kv_ref[:keys, HEAD:], grad, NT)
            probs = jnp.exp2(scores - lse_ref[row, cols])
            if mask is not None:
                probs = jnp.where(mask, probs, 0.0)
            dscores = (probs * (dprobs - delta_ref[row, cols])).astype(jnp.bfloat16)
            acc_ref[head, :, cols] += dot(keys_t, dscores, NN)
            probs_list.append(probs.astype(jnp.bfloat16))
            dscores_list.append(dscores)
            query_list.append(query)
            grad_list.append(grad)
        out_ref[:keys, :HEAD] += dot(
            jnp.concatenate(dscores_list, 1), jnp.concatenate(query_list, 0), NN
        )
        out_ref[:keys, HEAD:] += dot(
            jnp.concatenate(probs_list, 1), jnp.concatenate(grad_list, 0), NN
        )
        return 0

    lax.fori_loop(0, heads // JOIN, some, 0)


def grad_past_kernel(counts, first, seen_ref, first_ref, q_ref, g_ref, state_ref, delta_ref, *refs):
    total = sum(counts)
    kv_refs, rest = refs[:total], refs[total:]
    if first:
        acc_in = None
    else:
        acc_in, rest = rest[0], rest[1:]
    own_ref, other_ref, acc_ref, lse_ref, kv_all, keys_t_ref = rest
    rows = q_ref.shape[0]
    if first:
        acc_ref[...] = jnp.zeros(acc_ref.shape, jnp.float32)
    else:
        acc_ref[...] = acc_in[...]
    lse_ref[...] = lse_of(state_ref)
    for block in range(total):
        kv_all[block] = kv_refs[block][:rows, :]
    shared = (q_ref, g_ref, delta_ref, lse_ref, acc_ref)
    for offset, count, out_ref in ((0, counts[0], own_ref), (counts[0], counts[1], other_ref)):

        def one_block(at, _):
            block = at + offset
            seen, first_run = seen_ref[block], first_ref[0]
            out_ref[at] = jnp.zeros(out_ref.shape[1:], jnp.float32)
            kv_ref, block_out = kv_all.at[block], out_ref.at[at]

            @pl.when((seen > 0) & (first_run > 0))
            def _():
                keys_t_ref[...] = kv_ref[:, :HEAD].T

            for part in range(rows // QT):
                live = (seen > 0) & (first_run > part * QT)
                whole = (seen == rows) & (first_run >= (part + 1) * QT)

                @pl.when(live & whole)
                def _():
                    grad_tile(kv_ref, keys_t_ref[...], rows, None, part, shared, block_out)

                @pl.when(live & jnp.logical_not(whole))
                def _():
                    mask = past_mask(rows, rows - seen, first_run, part)
                    grad_tile(kv_ref, keys_t_ref[...], rows, mask, part, shared, block_out)

            return 0

        lax.fori_loop(0, count, one_block, 0)


def grad_own_kernel(local_ref, q_ref, g_ref, state_ref, delta_ref, kv_ref, acc_in, out_ref, dq_ref, acc_ref, lse_ref):
    rows = q_ref.shape[0]
    acc_ref[...] = acc_in[...]
    lse_ref[...] = lse_of(state_ref)
    out_ref[...] = jnp.zeros(out_ref.shape, jnp.float32)
    shared = (q_ref, g_ref, delta_ref, lse_ref, acc_ref)
    keys_t = kv_ref[:rows, :HEAD].T
    for part in range(rows // QT):
        upto = (part + 1) * QT
        mask = own_mask(local_ref, upto, part)
        grad_tile(kv_ref, keys_t[:, :upto], upto, mask, part, shared, out_ref)
    for head in range(acc_ref.shape[0]):
        dq_ref[:, head * HEAD : (head + 1) * HEAD] = (SCALE * acc_ref[head].T).astype(dq_ref.dtype)


def project_kernel(heads_ref, *refs):
    parts, (k_ref, v_ref, out_ref) = refs[:-3], refs[-3:]
    total = None
    for at, part_ref in enumerate(parts):
        lanes = head_lanes(heads_ref[at])
        weights = jnp.concatenate([k_ref[:, lanes], v_ref[:, lanes]], 1)
        add = dot(part_ref[...], weights, NT)
        total = add if total is None else total + add
    out_ref[...] = total.astype(out_ref.dtype)


SMEM = functools.partial(pl.BlockSpec, memory_space=pltpu.SMEM)
VMEM = functools.partial(pl.BlockSpec, memory_space=pltpu.VMEM)
PARAMS = pltpu.CompilerParams(vmem_limit_bytes=48 * 2**20)


def call(kernel, name, out_shape, args, smem, flops, moved, out_smem=(), scratch=()):
    one = not isinstance(out_shape, (tuple, list))
    shapes = (out_shape,) if one else tuple(out_shape)
    specs = tuple(SMEM() if at in out_smem else VMEM() for at in range(len(shapes)))
    return pl.pallas_call(
        kernel,
        out_shape=shapes[0] if one else shapes,
        in_specs=[SMEM() if at < smem else VMEM() for at in range(len(args))],
        out_specs=specs[0] if one else specs,
        scratch_shapes=list(scratch),
        compiler_params=PARAMS,
        cost_estimate=pl.CostEstimate(flops=int(flops), bytes_accessed=int(moved), transcendentals=0),
        name=name,
    )(*args)


def shift(value, steps):
    count = lax.axis_size("seq")
    return lax.ppermute(value, "seq", [(i, (i + steps) % count) for i in range(count)])


def swap(value):
    return lax.ppermute(value, "seq", [(i, i ^ 1) for i in range(lax.axis_size("seq"))])


def per_device(queries, keys, values, attn_out, out_grad, episode_ids, key_proj, value_proj):
    rows = queries.shape[0]
    group = queries.shape[1] // HEAD
    shard = lax.axis_index("seq")
    core = shard % 2
    f32 = jnp.float32
    unit = 4 * group * rows * rows * HEAD
    size = 2 * rows * HEAD

    kv = call(
        pack_kernel, "pack", jax.ShapeDtypeStruct((rows + META, 2 * HEAD), jnp.bfloat16),
        (episode_ids[None, :], keys, values), 0, size, 4 * size,
    )
    own = {0: kv}
    own[8] = shift(kv, 16)
    own[1] = shift(kv, 2)
    for near, far in ((2, 7), (3, 6)):
        own[near] = shift(own[near - 1], 2)
        own[far] = shift(own[far + 1], -2)
    own[4] = shift(own[3], 2)
    own[5] = shift(own[6], -2)
    other = {d: swap(own[d]) for d in range(9)}

    delta, norm = call(
        delta_kernel, "delta",
        (jax.ShapeDtypeStruct((group, rows), f32), jax.ShapeDtypeStruct((1,), f32)),
        (queries, out_grad, attn_out), 0, 1e9, 3 * group * size, out_smem=(1,),
    )
    local = jnp.sum(episode_ids[None, :] < episode_ids[:, None], 1, dtype=jnp.int32)[None, :]
    first_id = episode_ids[0]
    first_run = jnp.sum(episode_ids == first_id, dtype=jnp.int32)[None]

    def seen_of(blocks):
        meta = jnp.concatenate([block[rows : rows + 1, :HEAD] for block, _ in blocks], 0).astype(f32)
        places = jnp.stack([shard + step for _, step in blocks])
        past = (places >= 0) & (places < shard) & (meta[:, 0] == first_id.astype(f32))
        seen = jnp.where(past, (2 * meta[:, 1] + meta[:, 2]).astype(jnp.int32), 0)
        return seen, meta[:, 3]

    def owns(d):
        return own[d], -2 * d

    def others(d):
        return other[d], 1 - 2 * core - 2 * d

    state_shape = jax.ShapeDtypeStruct((3, group, rows), f32)
    state = call(
        stat_own_kernel, "stats_own", state_shape, (local, queries, kv), 0, unit, group * size
    )
    for distances in ((0, 1, 8, 2, 7), (3, 6, 4, 5)):
        blocks = []
        for d in distances:
            blocks += [others(d)] if d == 0 else [owns(d), others(d)]
        count = len(blocks)
        seen, key_norm = seen_of(blocks)
        state = call(
            functools.partial(stat_past_kernel, count), "stats", state_shape,
            (seen, first_run, key_norm, norm, queries, *(b for b, _ in blocks), state),
            4, count * unit, (count + group) * size,
            scratch=[pltpu.VMEM((count, rows, HEAD), jnp.bfloat16)],
        )

    acc = None
    far_sum = near_sum = sibling = None
    for far, near in ((5, 4), (6, 3), (7, 2), (8, 1)):
        mine = [owns(far), owns(near)]
        theirs = [others(far), others(near)] + ([others(0)] if near == 1 else [])
        seen, _ = seen_of(mine + theirs)
        count = len(mine) + len(theirs)
        args = (seen, first_run, queries, out_grad, state, delta, *(b for b, _ in mine + theirs))
        mine_out, their_out, acc = call(
            functools.partial(grad_past_kernel, (len(mine), len(theirs)), acc is None), "grads",
            (
                jax.ShapeDtypeStruct((len(mine), rows, 2 * HEAD), f32),
                jax.ShapeDtypeStruct((len(theirs), rows, 2 * HEAD), f32),
                jax.ShapeDtypeStruct((group, HEAD, rows), f32),
            ),
            args if acc is None else args + (acc,),
            2, 5 * count * unit, (4 * count + 6 * group) * size,
            scratch=[
                pltpu.VMEM((group, rows), f32),
                pltpu.VMEM((count, rows, 2 * HEAD), jnp.bfloat16),
                pltpu.VMEM((HEAD, rows), jnp.bfloat16),
            ],
        )
        swapped = swap(their_out)
        far_part = mine_out[0] + swapped[0]
        near_part = mine_out[1] + swapped[1]
        if far_sum is not None:
            far_part = far_part + far_sum.astype(f32)
            near_part = near_part + near_sum.astype(f32)
        far_sum = shift(far_part.astype(jnp.bfloat16), 2 if far < 8 else -16)
        near_sum = shift(near_part.astype(jnp.bfloat16), -2)
    sibling = swapped[2]
    part, query_grad = call(
        grad_own_kernel, "grads_own",
        (jax.ShapeDtypeStruct((rows, 2 * HEAD), f32), jax.ShapeDtypeStruct(queries.shape, jnp.bfloat16)),
        (local, queries, out_grad, state, delta, kv, acc), 0, 5 * unit, 6 * group * size,
        scratch=[pltpu.VMEM((group, HEAD, rows), f32), pltpu.VMEM((group, rows), f32)],
    )
    total = part + sibling + far_sum.astype(f32) + near_sum.astype(f32)
    is_key = jnp.arange(2 * HEAD) < HEAD
    total = jnp.where(is_key, SCALE, 1.0) * total
    both = total.astype(jnp.bfloat16)

    kv_heads = lax.axis_size("kvh")
    steps = list(range(kv_heads))
    parts = [both] + [
        lax.ppermute(both, "kvh", [(i, (i + step) % kv_heads) for i in range(kv_heads)])
        for step in steps[1:]
    ]
    heads = jnp.stack([(lax.axis_index("kvh") - step) % kv_heads for step in steps]).astype(jnp.int32)
    width = key_proj.shape[0]
    tile = 512
    input_grad = pl.pallas_call(
        project_kernel,
        grid=(width // tile,),
        out_shape=jax.ShapeDtypeStruct((rows, width), jnp.bfloat16),
        in_specs=[SMEM()]
        + [pl.BlockSpec((rows, 2 * HEAD), lambda n: (0, 0))] * len(parts)
        + [pl.BlockSpec((tile, key_proj.shape[1]), lambda n: (n, 0))] * 2,
        out_specs=pl.BlockSpec((rows, tile), lambda n: (0, n)),
        compiler_params=PARAMS,
        name="project",
    )(heads, *parts, key_proj, value_proj)
    return query_grad, both[:, :HEAD], both[:, HEAD:], input_grad


def solution(mesh):
    in_specs = (
        P("seq", "kvh"),
        P("seq", "kvh"),
        P("seq", "kvh"),
        P("seq", "kvh"),
        P("seq", "kvh"),
        P("seq"),
        P("kvh", None),
        P("kvh", None),
    )
    out_specs = (P("seq", "kvh"), P("seq", "kvh"), P("seq", "kvh"), P("seq", "kvh"))
    return jax.shard_map(
        per_device, mesh=mesh, in_specs=in_specs, out_specs=out_specs, check_vma=False
    )
```

```python
import functools
import jax
import jax.numpy as jnp
from jax import lax
from jax.experimental import pallas as pl
from jax.experimental.pallas import tpu as pltpu
from jax.sharding import PartitionSpec as P

HEAD = 128
LOG2E = 1.4426950408889634
SCALE = HEAD ** (-0.5)
GAIN = SCALE * LOG2E
NT = (((1,), (1,)), ((), ()))
NN = (((1,), (0,)), ((), ()))
TN = (((0,), (0,)), ((), ()))
QT = 256
JOIN = 4
META = 16
BOUND = 50.0


def dot(a, b, dims):
    return lax.dot_general(a, b, dims, preferred_element_type=jnp.float32)


def head_lanes(head):
    return pl.ds(pl.multiple_of(head * HEAD, HEAD), HEAD)


def pack_kernel(ids_ref, k_ref, v_ref, out_ref):
    rows = k_ref.shape[0]
    out_ref[:rows, :HEAD] = k_ref[...]
    out_ref[:rows, HEAD:] = v_ref[...]
    keys = k_ref[...].astype(jnp.float32)
    norm = 1.01 * jnp.max(jnp.sum(keys * keys, 1, keepdims=True))
    ids = ids_ref[...].astype(jnp.float32)
    last = jnp.max(ids)
    run = jnp.sum(jnp.where(ids == last, 1.0, 0.0)).astype(jnp.int32)
    lane = lax.broadcasted_iota(jnp.int32, (META, 2 * HEAD), 1)
    meta = jnp.where(lane == 0, last, jnp.where(lane == 1, (run >> 1).astype(jnp.float32), 0.0))
    meta = jnp.where(lane == 2, (run & 1).astype(jnp.float32), jnp.where(lane == 3, norm, meta))
    out_ref[rows:, :] = meta.astype(jnp.bfloat16)


def delta_kernel(q_ref, g_ref, o_ref, delta_ref, norm_ref):
    heads = delta_ref.shape[0]
    norm = jnp.float32(0.0)
    for head in range(heads):
        lanes = slice(head * HEAD, (head + 1) * HEAD)
        product = g_ref[:, lanes].astype(jnp.float32) * o_ref[:, lanes].astype(jnp.float32)
        high = product.astype(jnp.bfloat16)
        low = (product - high.astype(jnp.float32)).astype(jnp.bfloat16)
        both = jnp.concatenate([high, low], 1)
        delta_ref[head : head + 1, :] = dot(jnp.ones((16, 2 * HEAD), jnp.bfloat16), both, NT)[:1]
        query = q_ref[:, lanes].astype(jnp.float32)
        square = (query * query).astype(jnp.bfloat16)
        norm = jnp.maximum(norm, jnp.max(dot(jnp.ones((16, HEAD), jnp.bfloat16), square, NT)))
    norm_ref[0] = 1.02 * norm


def own_mask(local_ref, keys, part):
    shape = (keys, QT)
    place = lax.broadcasted_iota(jnp.int32, shape, 0)
    query = lax.broadcasted_iota(jnp.int32, shape, 1) + part * QT
    return (place >= local_ref[:, part * QT : (part + 1) * QT]) & (place <= query)


def past_mask(rows, low, first_run, part):
    shape = (rows, QT)
    place = lax.broadcasted_iota(jnp.int32, shape, 0)
    query = lax.broadcasted_iota(jnp.int32, shape, 1) + part * QT
    return (place >= low) & (query < first_run)


def stat_general(keys, mask, q_ref, part, state_ref, heads):
    cols = pl.ds(part * QT, QT)

    def one(head, _):
        row = pl.ds(head, 1)
        scores = GAIN * dot(keys, q_ref[cols, head_lanes(head)], NT)
        scores = jnp.where(mask, scores, -1e30)
        top = state_ref[0, row, cols]
        new_top = jnp.maximum(top, jnp.max(scores, 0, keepdims=True))
        add = jnp.sum(jnp.exp2(scores - new_top), 0, keepdims=True)
        add = jnp.where(new_top > -1e29, add, 0.0)
        state_ref[1, row, cols] = state_ref[1, row, cols] * jnp.exp2(top - new_top) + add
        state_ref[0, row, cols] = new_top
        return 0

    lax.fori_loop(0, heads, one, 0)


def stat_bounded(keys, q_ref, part, state_ref, heads):
    cols = pl.ds(part * QT, QT)

    def some(step, _):
        for at in range(JOIN):
            head = step * JOIN + at
            powers = jnp.exp2(GAIN * dot(keys, q_ref[cols, head_lanes(head)], NT))
            state_ref[2, pl.ds(head, 1), cols] += jnp.sum(powers, 0, keepdims=True)
        return 0

    lax.fori_loop(0, heads // JOIN, some, 0)


def stat_own_kernel(local_ref, q_ref, kv_ref, state_ref):
    heads, rows = state_ref.shape[1], state_ref.shape[2]
    state_ref[0] = jnp.full((heads, rows), -1e30, jnp.float32)
    state_ref[1] = jnp.zeros((heads, rows), jnp.float32)
    state_ref[2] = jnp.zeros((heads, rows), jnp.float32)
    for part in range(rows // QT):
        upto = (part + 1) * QT
        stat_general(
            kv_ref[:upto, :HEAD], own_mask(local_ref, upto, part), q_ref, part, state_ref, heads
        )


def stat_past_kernel(count, seen_ref, first_ref, key_norm_ref, norm_ref, q_ref, *refs):
    kv_refs, (state_in, state_ref, keys_ref) = refs[:count], refs[count:]
    heads, rows = state_ref.shape[1], state_ref.shape[2]
    state_ref[...] = state_in[...]
    for block in range(count):
        keys_ref[block] = kv_refs[block][:rows, :HEAD]

    def one_block(block, _):
        seen, first_run = seen_ref[block], first_ref[0]
        bounded = key_norm_ref[block] * norm_ref[0] * (GAIN * GAIN) < BOUND * BOUND
        for part in range(rows // QT):
            live = (seen > 0) & (first_run > part * QT)
            whole = (seen == rows) & (first_run >= (part + 1) * QT) & bounded

            @pl.when(live & whole)
            def _():
                stat_bounded(keys_ref[block], q_ref, part, state_ref, heads)

            @pl.when(live & jnp.logical_not(whole))
            def _():
                mask = past_mask(rows, rows - seen, first_run, part)
                stat_general(keys_ref[block], mask, q_ref, part, state_ref, heads)

        return 0

    lax.fori_loop(0, count, one_block, 0)


def lse_of(state_ref):
    top, total, flat = state_ref[0], state_ref[1], state_ref[2]
    flat_log = jnp.where(flat > 0, jnp.log2(jnp.where(flat > 0, flat, 1.0)), -1e30)
    high = jnp.maximum(top, flat_log)
    return high + jnp.log2(total * jnp.exp2(top - high) + jnp.exp2(flat_log - high))


def grad_tile(kv_ref, keys, mask, part, refs, out_ref):
    q_ref, g_ref, delta_ref, lse_ref, acc_ref = refs
    heads = lse_ref.shape[0]
    cols = pl.ds(part * QT, QT)

    def some(step, _):
        probs_list, dscores_list, query_list, grad_list = [], [], [], []
        for at in range(JOIN):
            head = step * JOIN + at
            row = pl.ds(head, 1)
            query = q_ref[cols, head_lanes(head)]
            grad = g_ref[cols, head_lanes(head)]
            scores = GAIN * dot(kv_ref[:keys, :HEAD], query, NT)
            dprobs = dot(kv_ref[:keys, HEAD:], grad, NT)
            probs = jnp.exp2(scores - lse_ref[row, cols])
            if mask is not None:
                probs = jnp.where(mask, probs, 0.0)
            dscores = (probs * (dprobs - delta_ref[row, cols])).astype(jnp.bfloat16)
            acc_ref[cols, head_lanes(head)] += dot(dscores, kv_ref[:keys, :HEAD], TN)
            probs_list.append(probs.astype(jnp.bfloat16))
            dscores_list.append(dscores)
            query_list.append(query)
            grad_list.append(grad)
        out_ref[:keys, :HEAD] += dot(
            jnp.concatenate(dscores_list, 1), jnp.concatenate(query_list, 0), NN
        )
        out_ref[:keys, HEAD:] += dot(
            jnp.concatenate(probs_list, 1), jnp.concatenate(grad_list, 0), NN
        )
        return 0

    lax.fori_loop(0, heads // JOIN, some, 0)


def grad_past_kernel(counts, first, seen_ref, first_ref, q_ref, g_ref, state_ref, delta_ref, *refs):
    total = sum(counts)
    kv_refs, rest = refs[:total], refs[total:]
    if first:
        acc_in = None
    else:
        acc_in, rest = rest[0], rest[1:]
    own_ref, other_ref, acc_ref, lse_ref, kv_all = rest
    rows = q_ref.shape[0]
    if first:
        acc_ref[...] = jnp.zeros(acc_ref.shape, jnp.float32)
    else:
        acc_ref[...] = acc_in[...]
    lse_ref[...] = lse_of(state_ref)
    for block in range(total):
        kv_all[block] = kv_refs[block][:rows, :]
    shared = (q_ref, g_ref, delta_ref, lse_ref, acc_ref)
    for offset, count, out_ref in ((0, counts[0], own_ref), (counts[0], counts[1], other_ref)):

        def one_block(at, _):
            block = at + offset
            seen, first_run = seen_ref[block], first_ref[0]
            out_ref[at] = jnp.zeros(out_ref.shape[1:], jnp.float32)
            kv_ref, block_out = kv_all.at[block], out_ref.at[at]

            for part in range(rows // QT):
                live = (seen > 0) & (first_run > part * QT)
                whole = (seen == rows) & (first_run >= (part + 1) * QT)

                @pl.when(live & whole)
                def _():
                    grad_tile(kv_ref, rows, None, part, shared, block_out)

                @pl.when(live & jnp.logical_not(whole))
                def _():
                    mask = past_mask(rows, rows - seen, first_run, part)
                    grad_tile(kv_ref, rows, mask, part, shared, block_out)

            return 0

        lax.fori_loop(0, count, one_block, 0)


def grad_own_kernel(local_ref, q_ref, g_ref, state_ref, delta_ref, kv_ref, acc_in, out_ref, dq_ref, acc_ref, lse_ref):
    rows = q_ref.shape[0]
    acc_ref[...] = acc_in[...]
    lse_ref[...] = lse_of(state_ref)
    out_ref[...] = jnp.zeros(out_ref.shape, jnp.float32)
    shared = (q_ref, g_ref, delta_ref, lse_ref, acc_ref)
    for part in range(rows // QT):
        upto = (part + 1) * QT
        mask = own_mask(local_ref, upto, part)
        grad_tile(kv_ref, upto, mask, part, shared, out_ref)
    dq_ref[...] = (SCALE * acc_ref[...]).astype(dq_ref.dtype)


def project_kernel(heads_ref, *refs):
    parts, (k_ref, v_ref, out_ref) = refs[:-3], refs[-3:]
    total = None
    for at, part_ref in enumerate(parts):
        lanes = head_lanes(heads_ref[at])
        weights = jnp.concatenate([k_ref[:, lanes], v_ref[:, lanes]], 1)
        add = dot(part_ref[...], weights, NT)
        total = add if total is None else total + add
    out_ref[...] = total.astype(out_ref.dtype)


SMEM = functools.partial(pl.BlockSpec, memory_space=pltpu.SMEM)
VMEM = functools.partial(pl.BlockSpec, memory_space=pltpu.VMEM)
PARAMS = pltpu.CompilerParams(vmem_limit_bytes=48 * 2**20)


def call(kernel, name, out_shape, args, smem, flops, moved, out_smem=(), scratch=()):
    one = not isinstance(out_shape, (tuple, list))
    shapes = (out_shape,) if one else tuple(out_shape)
    specs = tuple(SMEM() if at in out_smem else VMEM() for at in range(len(shapes)))
    return pl.pallas_call(
        kernel,
        out_shape=shapes[0] if one else shapes,
        in_specs=[SMEM() if at < smem else VMEM() for at in range(len(args))],
        out_specs=specs[0] if one else specs,
        scratch_shapes=list(scratch),
        compiler_params=PARAMS,
        cost_estimate=pl.CostEstimate(flops=int(flops), bytes_accessed=int(moved), transcendentals=0),
        name=name,
    )(*args)


def shift(value, steps):
    count = lax.axis_size("seq")
    return lax.ppermute(value, "seq", [(i, (i + steps) % count) for i in range(count)])


def swap(value):
    return lax.ppermute(value, "seq", [(i, i ^ 1) for i in range(lax.axis_size("seq"))])


def per_device(queries, keys, values, attn_out, out_grad, episode_ids, key_proj, value_proj):
    rows = queries.shape[0]
    group = queries.shape[1] // HEAD
    shard = lax.axis_index("seq")
    core = shard % 2
    f32 = jnp.float32
    unit = 4 * group * rows * rows * HEAD
    size = 2 * rows * HEAD

    kv = call(
        pack_kernel, "pack", jax.ShapeDtypeStruct((rows + META, 2 * HEAD), jnp.bfloat16),
        (episode_ids[None, :], keys, values), 0, size, 4 * size,
    )
    own = {0: kv}
    own[8] = shift(kv, 16)
    own[1] = shift(kv, 2)
    for near, far in ((2, 7), (3, 6)):
        own[near] = shift(own[near - 1], 2)
        own[far] = shift(own[far + 1], -2)
    own[4] = shift(own[3], 2)
    own[5] = shift(own[6], -2)
    other = {d: swap(own[d]) for d in range(9)}

    delta, norm = call(
        delta_kernel, "delta",
        (jax.ShapeDtypeStruct((group, rows), f32), jax.ShapeDtypeStruct((1,), f32)),
        (queries, out_grad, attn_out), 0, 1e9, 3 * group * size, out_smem=(1,),
    )
    local = jnp.sum(episode_ids[None, :] < episode_ids[:, None], 1, dtype=jnp.int32)[None, :]
    first_id = episode_ids[0]
    first_run = jnp.sum(episode_ids == first_id, dtype=jnp.int32)[None]

    def seen_of(blocks):
        meta = jnp.concatenate([block[rows : rows + 1, :HEAD] for block, _ in blocks], 0).astype(f32)
        places = jnp.stack([shard + step for _, step in blocks])
        past = (places >= 0) & (places < shard) & (meta[:, 0] == first_id.astype(f32))
        seen = jnp.where(past, (2 * meta[:, 1] + meta[:, 2]).astype(jnp.int32), 0)
        return seen, meta[:, 3]

    def owns(d):
        return own[d], -2 * d

    def others(d):
        return other[d], 1 - 2 * core - 2 * d

    state_shape = jax.ShapeDtypeStruct((3, group, rows), f32)
    state = call(
        stat_own_kernel, "stats_own", state_shape, (local, queries, kv), 0, unit, group * size
    )
    for distances in ((0, 1, 8, 2, 7), (3, 6, 4, 5)):
        blocks = []
        for d in distances:
            blocks += [others(d)] if d == 0 else [owns(d), others(d)]
        count = len(blocks)
        seen, key_norm = seen_of(blocks)
        state = call(
            functools.partial(stat_past_kernel, count), "stats", state_shape,
            (seen, first_run, key_norm, norm, queries, *(b for b, _ in blocks), state),
            4, count * unit, (count + group) * size,
            scratch=[pltpu.VMEM((count, rows, HEAD), jnp.bfloat16)],
        )

    acc = None
    far_sum = near_sum = None
    waits = []
    for far, near in ((5, 4), (6, 3), (7, 2), (8, 1)):
        if len(waits) > 1:
            acc, _ = lax.optimization_barrier((acc, waits[-2]))
        mine = [owns(far), owns(near)]
        theirs = [others(far), others(near)] + ([others(0)] if near == 1 else [])
        seen, _ = seen_of(mine + theirs)
        count = len(mine) + len(theirs)
        args = (seen, first_run, queries, out_grad, state, delta, *(b for b, _ in mine + theirs))
        mine_out, their_out, acc = call(
            functools.partial(grad_past_kernel, (len(mine), len(theirs)), acc is None), "grads",
            (
                jax.ShapeDtypeStruct((len(mine), rows, 2 * HEAD), f32),
                jax.ShapeDtypeStruct((len(theirs), rows, 2 * HEAD), f32),
                jax.ShapeDtypeStruct(queries.shape, f32),
            ),
            args if acc is None else args + (acc,),
            2, 5 * count * unit, (4 * count + 6 * group) * size,
            scratch=[
                pltpu.VMEM((group, rows), f32),
                pltpu.VMEM((count, rows, 2 * HEAD), jnp.bfloat16),
            ],
        )
        swapped = swap(their_out)
        far_part = mine_out[0] + swapped[0]
        near_part = mine_out[1] + swapped[1]
        if far_sum is not None:
            far_part = far_part + far_sum.astype(f32)
            near_part = near_part + near_sum.astype(f32)
        far_part, near_part = far_part.astype(jnp.bfloat16), near_part.astype(jnp.bfloat16)
        waits.append((far_part, near_part))
        far_sum = shift(far_part, 2 if far < 8 else -16)
        near_sum = shift(near_part, -2)
    sibling = swapped[2]
    acc, _ = lax.optimization_barrier((acc, waits[-1]))
    part, query_grad = call(
        grad_own_kernel, "grads_own",
        (jax.ShapeDtypeStruct((rows, 2 * HEAD), f32), jax.ShapeDtypeStruct(queries.shape, jnp.bfloat16)),
        (local, queries, out_grad, state, delta, kv, acc), 0, 5 * unit, 6 * group * size,
        scratch=[pltpu.VMEM(queries.shape, f32), pltpu.VMEM((group, rows), f32)],
    )
    total = part + sibling + far_sum.astype(f32) + near_sum.astype(f32)
    is_key = jnp.arange(2 * HEAD) < HEAD
    total = jnp.where(is_key, SCALE, 1.0) * total
    both = total.astype(jnp.bfloat16)

    kv_heads = lax.axis_size("kvh")
    steps = list(range(kv_heads))
    parts = [both] + [
        lax.ppermute(both, "kvh", [(i, (i + step) % kv_heads) for i in range(kv_heads)])
        for step in steps[1:]
    ]
    heads = jnp.stack([(lax.axis_index("kvh") - step) % kv_heads for step in steps]).astype(jnp.int32)
    width = key_proj.shape[0]
    tile = 512
    input_grad = pl.pallas_call(
        project_kernel,
        grid=(width // tile,),
        out_shape=jax.ShapeDtypeStruct((rows, width), jnp.bfloat16),
        in_specs=[SMEM()]
        + [pl.BlockSpec((rows, 2 * HEAD), lambda n: (0, 0))] * len(parts)
        + [pl.BlockSpec((tile, key_proj.shape[1]), lambda n: (n, 0))] * 2,
        out_specs=pl.BlockSpec((rows, tile), lambda n: (0, n)),
        compiler_params=PARAMS,
        name="project",
    )(heads, *parts, key_proj, value_proj)
    return query_grad, both[:, :HEAD], both[:, HEAD:], input_grad


def solution(mesh):
    in_specs = (
        P("seq", "kvh"),
        P("seq", "kvh"),
        P("seq", "kvh"),
        P("seq", "kvh"),
        P("seq", "kvh"),
        P("seq"),
        P("kvh", None),
        P("kvh", None),
    )
    out_specs = (P("seq", "kvh"), P("seq", "kvh"), P("seq", "kvh"), P("seq", "kvh"))
    return jax.shard_map(
        per_device, mesh=mesh, in_specs=in_specs, out_specs=out_specs, check_vma=False
    )
```

```python
import functools
import jax
import jax.numpy as jnp
from jax import lax
from jax.experimental import pallas as pl
from jax.experimental.pallas import tpu as pltpu
from jax.sharding import PartitionSpec as P

HEAD = 128
LOG2E = 1.4426950408889634
SCALE = HEAD ** (-0.5)
GAIN = SCALE * LOG2E
NT = (((1,), (1,)), ((), ()))
NN = (((1,), (0,)), ((), ()))
QT = 256
JOIN = 4
NEAR = 4
FAR = 4
META = 16
BOUND = 50.0


def dot(a, b, dims):
    return lax.dot_general(a, b, dims, preferred_element_type=jnp.float32)


def head_lanes(head):
    return pl.ds(pl.multiple_of(head * HEAD, HEAD), HEAD)


def pack_kernel(ids_ref, k_ref, v_ref, out_ref):
    rows = k_ref.shape[0]
    out_ref[:rows, :HEAD] = k_ref[...]
    out_ref[:rows, HEAD:] = v_ref[...]
    keys = k_ref[...].astype(jnp.float32)
    norm = 1.01 * jnp.max(jnp.sum(keys * keys, 1, keepdims=True))
    ids = ids_ref[...].astype(jnp.float32)
    last = jnp.max(ids)
    run = jnp.sum(jnp.where(ids == last, 1.0, 0.0)).astype(jnp.int32)
    lane = lax.broadcasted_iota(jnp.int32, (META, 2 * HEAD), 1)
    meta = jnp.where(lane == 0, last, jnp.where(lane == 1, (run >> 1).astype(jnp.float32), 0.0))
    meta = jnp.where(lane == 2, (run & 1).astype(jnp.float32), jnp.where(lane == 3, norm, meta))
    out_ref[rows:, :] = meta.astype(jnp.bfloat16)


def delta_kernel(q_ref, g_ref, o_ref, delta_ref, norm_ref):
    heads = delta_ref.shape[0]
    norm = jnp.float32(0.0)
    for head in range(heads):
        lanes = slice(head * HEAD, (head + 1) * HEAD)
        product = g_ref[:, lanes].astype(jnp.float32) * o_ref[:, lanes].astype(jnp.float32)
        high = product.astype(jnp.bfloat16)
        low = (product - high.astype(jnp.float32)).astype(jnp.bfloat16)
        both = jnp.concatenate([high, low], 1)
        delta_ref[head : head + 1, :] = dot(jnp.ones((16, 2 * HEAD), jnp.bfloat16), both, NT)[:1]
        query = q_ref[:, lanes].astype(jnp.float32)
        square = (query * query).astype(jnp.bfloat16)
        norm = jnp.maximum(norm, jnp.max(dot(jnp.ones((16, HEAD), jnp.bfloat16), square, NT)))
    norm_ref[0] = 1.02 * norm


def own_mask(local_ref, keys, part):
    shape = (keys, QT)
    place = lax.broadcasted_iota(jnp.int32, shape, 0)
    query = lax.broadcasted_iota(jnp.int32, shape, 1) + part * QT
    return (place >= local_ref[:, part * QT : (part + 1) * QT]) & (place <= query)


def past_mask(rows, low):
    return lax.broadcasted_iota(jnp.int32, (rows, QT), 0) >= low


def stat_general(keys, mask, q_ref, part, state_ref, heads):
    cols = pl.ds(part * QT, QT)

    def one(head, _):
        row = pl.ds(head, 1)
        scores = GAIN * dot(keys, q_ref[cols, head_lanes(head)], NT)
        scores = jnp.where(mask, scores, -1e30)
        top = state_ref[0, row, cols]
        new_top = jnp.maximum(top, jnp.max(scores, 0, keepdims=True))
        add = jnp.sum(jnp.exp2(scores - new_top), 0, keepdims=True)
        add = jnp.where(new_top > -1e29, add, 0.0)
        state_ref[1, row, cols] = state_ref[1, row, cols] * jnp.exp2(top - new_top) + add
        state_ref[0, row, cols] = new_top
        return 0

    lax.fori_loop(0, heads, one, 0)


def stat_bounded(keys, first_run, q_ref, part, state_ref, heads):
    cols = pl.ds(part * QT, QT)
    sees = lax.broadcasted_iota(jnp.int32, (1, QT), 1) + part * QT < first_run

    def some(step, _):
        for at in range(JOIN):
            head = step * JOIN + at
            powers = jnp.exp2(GAIN * dot(keys, q_ref[cols, head_lanes(head)], NT))
            add = jnp.where(sees, jnp.sum(powers, 0, keepdims=True), 0.0)
            state_ref[2, pl.ds(head, 1), cols] += add
        return 0

    lax.fori_loop(0, heads // JOIN, some, 0)


def clear(state_ref):
    state_ref[0] = jnp.full(state_ref.shape[1:], -1e30, jnp.float32)
    state_ref[1] = jnp.zeros(state_ref.shape[1:], jnp.float32)
    state_ref[2] = jnp.zeros(state_ref.shape[1:], jnp.float32)


def stat_own_kernel(local_ref, q_ref, kv_ref, state_ref):
    heads, rows = state_ref.shape[1], state_ref.shape[2]
    clear(state_ref)
    for part in range(rows // QT):
        upto = (part + 1) * QT
        stat_general(
            kv_ref[:upto, :HEAD], own_mask(local_ref, upto, part), q_ref, part, state_ref, heads
        )


def stat_past_kernel(count, seen_ref, first_ref, key_norm_ref, norm_ref, q_ref, *refs):
    kv_refs, rest = refs[:count], refs[count:]
    state_ref, keys_ref = rest[-2:]
    heads, rows = state_ref.shape[1], state_ref.shape[2]
    if len(rest) == 3:
        state_ref[...] = rest[0][...]
    else:
        clear(state_ref)
    for block in range(count):
        keys_ref[block] = kv_refs[block][:rows, :HEAD]

    def one_block(block, _):
        seen, first_run = seen_ref[block], first_ref[0]
        bounded = key_norm_ref[block] * norm_ref[0] * (GAIN * GAIN) < BOUND * BOUND
        for part in range(rows // QT):
            live = (seen > 0) & (first_run > part * QT)
            whole = (seen == rows) & bounded

            @pl.when(live & whole)
            def _():
                stat_bounded(keys_ref[block], first_run, q_ref, part, state_ref, heads)

            @pl.when(live & jnp.logical_not(whole))
            def _():
                query = lax.broadcasted_iota(jnp.int32, (rows, QT), 1) + part * QT
                mask = past_mask(rows, rows - seen) & (query < first_run)
                stat_general(keys_ref[block], mask, q_ref, part, state_ref, heads)

        return 0

    lax.fori_loop(0, count, one_block, 0)


def lse_of(states):
    terms = []
    for state in states:
        flat = state[2]
        terms.append((state[0], state[1]))
        terms.append((jnp.where(flat > 0, jnp.log2(jnp.where(flat > 0, flat, 1.0)), -1e30), 1.0))
    high = functools.reduce(jnp.maximum, [top for top, _ in terms])
    return high + jnp.log2(sum(part * jnp.exp2(top - high) for top, part in terms))


def grad_tile(kv_ref, keys_t, keys, mask, part, refs, out_ref):
    q_ref, g_ref, delta_ref, lse_ref, acc_ref = refs
    heads = lse_ref.shape[0]
    cols = pl.ds(part * QT, QT)

    def some(step, _):
        probs_list, dscores_list, query_list, grad_list = [], [], [], []
        for at in range(JOIN):
            head = step * JOIN + at
            row = pl.ds(head, 1)
            query = q_ref[cols, head_lanes(head)]
            grad = g_ref[cols, head_lanes(head)]
            scores = GAIN * dot(kv_ref[:keys, :HEAD], query, NT)
            dprobs = dot(kv_ref[:keys, HEAD:], grad, NT)
            probs = jnp.exp2(scores - lse_ref[row, cols])
            if mask is not None:
                probs = jnp.where(mask, probs, 0.0)
            dscores = (probs * (dprobs - delta_ref[row, cols])).astype(jnp.bfloat16)
            acc_ref[head, :, cols] += dot(keys_t, dscores, NN)
            probs_list.append(probs.astype(jnp.bfloat16))
            dscores_list.append(dscores)
            query_list.append(query)
            grad_list.append(grad)
        out_ref[:keys, :HEAD] += dot(
            jnp.concatenate(dscores_list, 1), jnp.concatenate(query_list, 0), NN
        )
        out_ref[:keys, HEAD:] += dot(
            jnp.concatenate(probs_list, 1), jnp.concatenate(grad_list, 0), NN
        )
        return 0

    lax.fori_loop(0, heads // JOIN, some, 0)


def grad_past_kernel(counts, first, far, seen_ref, first_ref, q_ref, g_ref, lse_ref, delta_ref, *refs):
    total = sum(counts)
    kv_refs, rest = refs[:total], refs[total:]
    acc_in = None
    if not first:
        acc_in, rest = rest[0], rest[1:]
    own_ref, other_ref, acc_ref, kv_all, keys_t_ref = rest[:5]
    sum_ref = rest[5] if far else acc_ref
    rows = q_ref.shape[0]
    if first:
        sum_ref[...] = jnp.zeros(sum_ref.shape, jnp.float32)
    else:
        sum_ref[...] = acc_in[...]
    for block in range(total):
        kv_all[block] = kv_refs[block][:rows, :]
    shared = (q_ref, g_ref, delta_ref, lse_ref, sum_ref)
    for offset, count, out_ref in ((0, counts[0], own_ref), (counts[0], counts[1], other_ref)):

        def one_block(at, _):
            block = at + offset
            seen, first_run = seen_ref[block], first_ref[0]
            out_ref[at] = jnp.zeros(out_ref.shape[1:], jnp.float32)
            kv_ref, block_out = kv_all.at[block], out_ref.at[at]

            @pl.when((seen > 0) & (first_run > 0))
            def _():
                keys_t_ref[...] = kv_ref[:, :HEAD].T

            for part in range(rows // QT):
                live = (seen > 0) & (first_run > part * QT)

                @pl.when(live & (seen == rows))
                def _():
                    grad_tile(kv_ref, keys_t_ref[...], rows, None, part, shared, block_out)

                @pl.when(live & (seen < rows))
                def _():
                    mask = past_mask(rows, rows - seen)
                    grad_tile(kv_ref, keys_t_ref[...], rows, mask, part, shared, block_out)

            return 0

        lax.fori_loop(0, count, one_block, 0)
    if far:
        acc_ref[...] = sum_ref[...].astype(acc_ref.dtype)


def grad_own_kernel(local_ref, q_ref, g_ref, lse_ref, delta_ref, kv_ref, acc_in, far_in, out_ref, dq_ref, acc_ref):
    rows = q_ref.shape[0]
    acc_ref[...] = acc_in[...] + far_in[...].astype(jnp.float32)
    out_ref[...] = jnp.zeros(out_ref.shape, jnp.float32)
    shared = (q_ref, g_ref, delta_ref, lse_ref, acc_ref)
    keys_t = kv_ref[:rows, :HEAD].T
    for part in range(rows // QT):
        upto = (part + 1) * QT
        mask = own_mask(local_ref, upto, part)
        grad_tile(kv_ref, keys_t[:, :upto], upto, mask, part, shared, out_ref)
    for head in range(acc_ref.shape[0]):
        dq_ref[:, head * HEAD : (head + 1) * HEAD] = (SCALE * acc_ref[head].T).astype(dq_ref.dtype)


def project_kernel(heads_ref, *refs):
    parts, (k_ref, v_ref, out_ref) = refs[:-3], refs[-3:]
    total = None
    for at, part_ref in enumerate(parts):
        lanes = head_lanes(heads_ref[at])
        weights = jnp.concatenate([k_ref[:, lanes], v_ref[:, lanes]], 1)
        add = dot(part_ref[...], weights, NT)
        total = add if total is None else total + add
    out_ref[...] = total.astype(out_ref.dtype)


SMEM = functools.partial(pl.BlockSpec, memory_space=pltpu.SMEM)
VMEM = functools.partial(pl.BlockSpec, memory_space=pltpu.VMEM)
PARAMS = pltpu.CompilerParams(vmem_limit_bytes=48 * 2**20)


def call(kernel, name, out_shape, args, smem, flops, moved, out_smem=(), scratch=()):
    one = not isinstance(out_shape, (tuple, list))
    shapes = (out_shape,) if one else tuple(out_shape)
    specs = tuple(SMEM() if at in out_smem else VMEM() for at in range(len(shapes)))
    return pl.pallas_call(
        kernel,
        out_shape=shapes[0] if one else shapes,
        in_specs=[SMEM() if at < smem else VMEM() for at in range(len(args))],
        out_specs=specs[0] if one else specs,
        scratch_shapes=list(scratch),
        compiler_params=PARAMS,
        cost_estimate=pl.CostEstimate(flops=int(flops), bytes_accessed=int(moved), transcendentals=0),
        name=name,
    )(*args)


def shift(value, steps):
    count = lax.axis_size("seq")
    return lax.ppermute(value, "seq", [(i, (i + steps) % count) for i in range(count)])


def swap(value):
    return lax.ppermute(value, "seq", [(i, i ^ 1) for i in range(lax.axis_size("seq"))])


def per_device(queries, keys, values, attn_out, out_grad, episode_ids, key_proj, value_proj):
    rows = queries.shape[0]
    group = queries.shape[1] // HEAD
    shard = lax.axis_index("seq")
    core = shard % 2
    f32 = jnp.float32
    unit = 4 * group * rows * rows * HEAD
    size = 2 * rows * HEAD

    kv = call(
        pack_kernel, "pack", jax.ShapeDtypeStruct((rows + META, 2 * HEAD), jnp.bfloat16),
        (episode_ids[None, :], keys, values), 0, size, 4 * size,
    )
    own = {0: kv}
    for d in range(1, NEAR + 1):
        own[d] = shift(own[d - 1], 2)
        if d < FAR:
            own[-d] = shift(own[1 - d], -2)
    other = {d: swap(own[d]) for d in own}
    away = 2 * (NEAR + FAR)
    info = jnp.stack([episode_ids[0], jnp.sum(episode_ids == episode_ids[0], dtype=jnp.int32)])
    far_info = shift(info, -away)
    far_queries = shift(queries, -away)
    held, _ = lax.optimization_barrier((out_grad, far_queries))
    far_grad = shift(held, -away)

    delta, norm = call(
        delta_kernel, "delta",
        (jax.ShapeDtypeStruct((group, rows), f32), jax.ShapeDtypeStruct((1,), f32)),
        (queries, out_grad, attn_out), 0, 1e9, 3 * group * size, out_smem=(1,),
    )
    local = jnp.sum(episode_ids[None, :] < episode_ids[:, None], 1, dtype=jnp.int32)[None, :]
    first_run = info[1:]
    far_first_run = far_info[1:]
    far_shard = (shard + away) % lax.axis_size("seq")

    def seen_of(blocks, first_id):
        meta = jnp.concatenate([block[rows : rows + 1, :HEAD] for block, _ in blocks], 0).astype(f32)
        there = jnp.stack([valid for _, valid in blocks])
        past = there & (meta[:, 0] == first_id.astype(f32))
        seen = jnp.where(past, (2 * meta[:, 1] + meta[:, 2]).astype(jnp.int32), 0)
        return seen, meta[:, 3]

    def blocks_of(table, distances):
        found = []
        for d in distances:
            step = 0 if table is own else 1 - 2 * core
            place = shard + step - 2 * d
            found.append((table[d], (place >= 0) & (place < shard if d >= 0 else True)))
        return found

    def far_blocks(table):
        step = 0 if table is own else 1 - 2 * core
        return [(table[-j], far_shard - away + 2 * j + step >= 0) for j in range(FAR - 1, -1, -1)]

    state_shape = jax.ShapeDtypeStruct((3, group, rows), f32)

    def stats(blocks, run, first_id, rows_of, key_limit, state):
        count = len(blocks)
        seen, key_norm = seen_of(blocks, first_id)
        extra = () if state is None else (state,)
        return seen, call(
            functools.partial(stat_past_kernel, count), "stats", state_shape,
            (seen, run, key_norm, key_limit, rows_of, *(b for b, _ in blocks), *extra),
            4, count * unit, (count + group) * size,
            scratch=[pltpu.VMEM((count, rows, HEAD), jnp.bfloat16)],
        )

    state = call(
        stat_own_kernel, "stats_own", state_shape, (local, queries, kv), 0, unit, group * size
    )
    far_norm = shift(norm, -away)
    far_list = far_blocks(own) + far_blocks(other)
    far_seen, far_state = stats(far_list, far_first_run, far_info[0], far_queries, far_norm, None)
    far_state = shift(far_state, away)
    near_steps = tuple(range(NEAR, 0, -1))
    near_list = blocks_of(own, near_steps) + blocks_of(other, near_steps + (0,))
    near_seen, state = stats(near_list, first_run, info[0], queries, norm, state)
    lse = lse_of((state, far_state))
    past_lse = jnp.where(jnp.arange(rows) < first_run[0], lse, 1e30)
    far_rows = shift(jnp.stack([past_lse, delta]), -away)

    def grads(mine, theirs, seen, run, rows_of, grad_of, lse_rows, delta_rows, acc, far, last):
        count = len(mine) + len(theirs)
        extra = () if acc is None else (acc,)
        scratch = [
            pltpu.VMEM((count, rows, 2 * HEAD), jnp.bfloat16),
            pltpu.VMEM((HEAD, rows), jnp.bfloat16),
        ]
        if last:
            scratch.append(pltpu.VMEM((group, HEAD, rows), f32))
        return call(
            functools.partial(grad_past_kernel, (len(mine), len(theirs)), acc is None, last),
            "grads_far" if far else "grads_near",
            (
                jax.ShapeDtypeStruct((len(mine), rows, 2 * HEAD), f32),
                jax.ShapeDtypeStruct((len(theirs), rows, 2 * HEAD), f32),
                jax.ShapeDtypeStruct((group, HEAD, rows), jnp.bfloat16 if last else f32),
            ),
            (seen, run, rows_of, grad_of, lse_rows, delta_rows, *(b for b, _ in mine + theirs), *extra),
            2, 5 * count * unit, (4 * count + 6 * group) * size, scratch=scratch,
        )

    def pick(seen, places):
        return jnp.stack([seen[place] for place in places])

    def relay(parts, carried, step):
        for part in parts:
            part = part if carried is None else part + carried.astype(f32)
            carried = shift(part.astype(jnp.bfloat16), step)
        return carried

    bf16 = jnp.bfloat16
    lot = NEAR - 1
    mine, theirs = near_list[:lot], near_list[NEAR : NEAR + lot]
    seen = pick(near_seen, list(range(lot)) + list(range(NEAR, NEAR + lot)))
    mine_out, their_out, acc = grads(
        mine, theirs, seen, first_run, queries, out_grad, past_lse, delta, None, False, False
    )
    moved = swap(their_out)
    near_parts = [mine_out[at] + moved[at] for at in range(lot)]

    half = FAR // 2
    far_acc, far_sum, far_total = None, None, None
    for turn in range(2):
        picked = list(range(turn * half, (turn + 1) * half))
        mine = [far_list[at] for at in picked]
        theirs = [far_list[FAR + at] for at in picked]
        seen = pick(far_seen, picked + [FAR + at for at in picked])
        mine_out, their_out, far_acc = grads(
            mine, theirs, seen, far_first_run, far_queries, far_grad, far_rows[0], far_rows[1],
            far_acc, True, turn == 1,
        )
        moved = swap(their_out)
        far_parts = [mine_out[at] + moved[at] for at in range(half)]
        if turn == 0:
            near_sum = relay(near_parts, None, -2)
            far_sum = relay(far_parts, None, 2)
        else:
            far_sum = relay(far_parts[:-1], far_sum, 2)
            far_total = far_parts[-1] + far_sum.astype(f32)
    far_acc = shift(far_acc, away)

    mine, theirs = near_list[lot:NEAR], near_list[NEAR + lot :]
    seen = pick(near_seen, [lot] + list(range(NEAR + lot, 2 * NEAR + 1)))
    acc, near_sum, _ = lax.optimization_barrier((acc, near_sum, far_parts))
    mine_out, their_out, acc = grads(
        mine, theirs, seen, first_run, queries, out_grad, past_lse, delta, acc, False, False
    )
    moved = swap(their_out)
    near_sum = relay([mine_out[0] + moved[0]], near_sum, -2)
    acc, far_total = lax.optimization_barrier((acc, far_total))
    part, query_grad = call(
        grad_own_kernel, "grads_own",
        (jax.ShapeDtypeStruct((rows, 2 * HEAD), f32), jax.ShapeDtypeStruct(queries.shape, bf16)),
        (local, queries, out_grad, lse, delta, kv, acc, far_acc), 0, 5 * unit, 6 * group * size,
        scratch=[pltpu.VMEM((group, HEAD, rows), f32)],
    )
    total = part + moved[1] + far_total + near_sum.astype(f32)
    is_key = jnp.arange(2 * HEAD) < HEAD
    total = jnp.where(is_key, SCALE, 1.0) * total
    both = total.astype(bf16)

    kv_heads = lax.axis_size("kvh")
    steps = list(range(kv_heads))
    parts = [both] + [
        lax.ppermute(both, "kvh", [(i, (i + step) % kv_heads) for i in range(kv_heads)])
        for step in steps[1:]
    ]
    heads = jnp.stack([(lax.axis_index("kvh") - step) % kv_heads for step in steps]).astype(jnp.int32)
    width = key_proj.shape[0]
    tile = 512
    input_grad = pl.pallas_call(
        project_kernel,
        grid=(width // tile,),
        out_shape=jax.ShapeDtypeStruct((rows, width), jnp.bfloat16),
        in_specs=[SMEM()]
        + [pl.BlockSpec((rows, 2 * HEAD), lambda n: (0, 0))] * len(parts)
        + [pl.BlockSpec((tile, key_proj.shape[1]), lambda n: (n, 0))] * 2,
        out_specs=pl.BlockSpec((rows, tile), lambda n: (0, n)),
        compiler_params=PARAMS,
        name="project",
    )(heads, *parts, key_proj, value_proj)
    return query_grad, both[:, :HEAD], both[:, HEAD:], input_grad


def solution(mesh):
    in_specs = (
        P("seq", "kvh"),
        P("seq", "kvh"),
        P("seq", "kvh"),
        P("seq", "kvh"),
        P("seq", "kvh"),
        P("seq"),
        P("kvh", None),
        P("kvh", None),
    )
    out_specs = (P("seq", "kvh"), P("seq", "kvh"), P("seq", "kvh"), P("seq", "kvh"))
    return jax.shard_map(
        per_device, mesh=mesh, in_specs=in_specs, out_specs=out_specs, check_vma=False
    )
```
